256 devices in a mesh: ctx: 32 (over y, z), tp: 8 (over x, core).
Axes of the slice: x: 4, y: 4, z: 8, core: 2. Of those that a mesh axis runs over, the one named last changes fastest.
Arguments:
- lengths: int32 [32], replicated, may hold values from 1 to 4096, 8192 in all
- queries: bfloat16 [8192, 2048], P('ctx', 'tp'), may hold values from -150 to 150
- keys: bfloat16 [8192, 1024], P('ctx', 'tp'), may hold values from -8 to 8
- values: bfloat16 [8192, 1024], P('ctx', 'tp'), may hold values from -6 to 6
- ssm_input: bfloat16 [8192, 4096], P('ctx', 'tp'), may hold values from -6 to 6
- gate_input: bfloat16 [8192, 4096], P('ctx', 'tp'), may hold values from -6 to 6
- b_input: bfloat16 [8192, 1024], P('ctx', 'tp'), may hold values from -1.25 to 1.25
- c_input: bfloat16 [8192, 1024], P('ctx', 'tp'), may hold values from -6 to 6
- log_decay: float32 [8192, 64], P('ctx', 'tp'), may hold values from -1 to 0
- skip: float32 [64], P('tp'), may hold values from 0.5 to 2
- norm_gain: float32 [4096], P('tp'), may hold values from 0.5 to 1.5
- attn_out_weight: bfloat16 [2048, 5120], P('tp'), may hold values from -0.125 to 0.125
- ssm_out_weight: bfloat16 [4096, 5120], P('tp'), may hold values from -0.09375 to 0.09375
- cotangent: bfloat16 [8192, 5120], P('ctx', 'tp'), may hold values from -6 to 6
Outputs:
- mixed: bfloat16 [8192, 5120], P('ctx', 'tp')
- grad_attn_out: float32 [5120, 2048], P('ctx', 'tp')
- grad_ssm_out: float32 [5120, 4096], P('ctx', 'tp')
The draws below stay inside these ranges and needn't reach their ends.
Inputs may be any that keep to these rules, and one draw needn't show every extreme that they name: `lengths`: they sum to 8192 and the longest is exactly 4096.
All inputs are finite; a program needn't handle non-finite values.
Results may differ from the reference program's by a relative error of at most 0.025.
Values may be sent and summed in bfloat16 or wider, within the bound.
No kernel may reach another device: no remote copies, remote signals or barrier semaphores. Data moves between devices by JAX's collectives and lax.ppermute only.
A program may use at most 128 MiB of HBM per device.

```python
import math
import jax
import jax.numpy as jnp
import numpy as np
from jax import lax

D = 5120
QH = 16
KEY_VALUE_HEADS = 8
HEAD_SIZE = 128
SH = 64
SP = 64
SN = 128
G = 8
TOKENS_PER_PARTITION = 256
SEQUENCE_LENGTH = 8192
DOC_MOST = 4096
VISIBLE_BLOCKS = 16
NDOC = 32
HID = 6144
N_CTX = 32
N_TP = 8


def shared_keys(key):
    return jax.random.normal(jax.random.fold_in(key, 101), (SEQUENCE_LENGTH, KEY_VALUE_HEADS * HEAD_SIZE), jnp.float32)


def draw_keys(key, part):
    base = shared_keys(key)
    return jnp.clip(base, -7.5, 7.5).astype(jnp.bfloat16)


def draw_queries(key, part):
    key = jax.random.fold_in(key, 3)
    fresh = jax.random.normal(key, (SEQUENCE_LENGTH, QH * HEAD_SIZE), jnp.float32)
    fresh = jnp.clip(fresh, -7.5, 7.5)
    return fresh.astype(jnp.bfloat16)


def draw_log_decay(key, part):
    key = jax.random.fold_in(key, 7)
    keys = jax.random.split(key, 7)
    fast = jax.random.bernoulli(keys[1], 0.5, (SH,))
    quick = jnp.exp(jax.random.uniform(keys[0], (SH,), jnp.float32, jnp.log(1.0 / 50.0), jnp.log(1.0 / 30.0)))
    slow = jnp.exp(jax.random.uniform(keys[6], (SH,), jnp.float32, jnp.log(0.2 / DOC_MOST), jnp.log(2.0 / DOC_MOST)))
    decay_rate = jnp.where(fast, quick, slow)
    jitter = jax.random.uniform(keys[2], (SEQUENCE_LENGTH, SH), jnp.float32, 0.5, 1.5)
    block_scale = jax.random.uniform(keys[3], (SEQUENCE_LENGTH // TOKENS_PER_PARTITION, 1, SH), jnp.float32, 0.6, 1.4)
    block_scale = jnp.broadcast_to(block_scale, (SEQUENCE_LENGTH // TOKENS_PER_PARTITION, TOKENS_PER_PARTITION, SH)).reshape(SEQUENCE_LENGTH, SH)
    spike_positions = jax.random.randint(keys[4], (8,), 0, SEQUENCE_LENGTH)
    is_spike = jnp.any(jnp.arange(SEQUENCE_LENGTH)[:, None] == spike_positions[None, :], axis=1)[:, None]
    spike_log = jnp.log(jax.random.uniform(keys[5], (SEQUENCE_LENGTH, 1), jnp.float32, 0.5, 0.8))
    log_decay = -decay_rate[None, :] * jitter * block_scale + jnp.where(is_spike, spike_log, 0.0)
    return jnp.clip(log_decay, -1.0, 0.0).astype(jnp.float32)


def spiked(entries, key, source, target, parts, factor):
    owner, partner = [(jnp.arange(entries.shape[dim]) // (entries.shape[dim] // parts)).reshape([-1 if axis == dim else 1 for axis in range(entries.ndim)]) for dim in (source, target)]
    chosen = jax.random.permutation(key, parts)[partner]
    strong = (owner == chosen) | (owner == (partner + parts // 2) % parts)
    return jnp.where(strong, factor * entries, entries)


def shard_levels(key, extent, cuts, low, high):
    level = 1.0
    for dim, blocks in cuts:
        heights = jax.random.uniform(jax.random.fold_in(jax.random.fold_in(key, 6), dim), (blocks,), jnp.float32, low / len(cuts), high / len(cuts))
        level = level * jnp.repeat(jnp.exp(heights), extent[dim] // blocks).reshape((-1,) + (1,) * (len(extent) - 1 - dim))
    return level


def profile(count, total, reach, lean):
    portions = [(1 << 20) // math.isqrt(rank ** lean) + 1 for rank in range(2, count + 1)]
    rest, counts = total - reach - (count - 1), [1] * (count - 1)
    while rest > 0:
        free = [i for i in range(count - 1) if counts[i] < reach]
        mass, left = sum([portions[i] for i in free]), rest
        for i in free:
            addition = min(reach - counts[i], max(1, left * portions[i] // mass), rest)
            counts[i] = counts[i] + addition
            rest = rest - addition
    return np.array([reach] + counts)


def uneven(own_key, amount, total, limit, lean):
    if amount == 2:
        one = jax.random.randint(own_key, (), max(1, total - limit), min(limit, total - 1) + 1)
        return jnp.stack([one, total - one])
    tallies = jnp.asarray(profile(amount, total, limit, lean), jnp.int32)
    twos = (amount - 1) // 2
    giver, receiver = tallies[1:1 + 2 * twos:2], tallies[2:2 + 2 * twos:2]
    margin = jnp.minimum(giver - 1, limit - receiver)
    shifted = jax.random.randint(jax.random.fold_in(own_key, 1), (twos,), 0, 1 << 20) % (margin + 1)
    tallies = tallies.at[1:1 + 2 * twos:2].set(giver - shifted).at[2:2 + 2 * twos:2].set(receiver + shifted)
    return tallies[jax.random.permutation(jax.random.fold_in(own_key, 2), amount)]


def gaussian(own_key, shape, width, reach, pieces=(), held_as=jnp.bfloat16):
    result = width * jax.random.normal(own_key, shape, jnp.float32)
    if pieces:
        result = result * shard_levels(own_key, shape, pieces, -0.22, 0.18)
    return jnp.clip(result, -reach, reach).astype(held_as)


def bell_draw_with(key, shape, width, most, shards, heavy, held_as=jnp.bfloat16):
    array = width * jax.random.normal(key, shape, jnp.float32)
    if shards:
        array = array * shard_levels(key, shape, shards, -0.22, 0.18)
    return jnp.clip(spiked(array, jax.random.fold_in(key, 3), *heavy), -most, most).astype(held_as)


def setup_inputs(seed: int = 0) -> dict:
    key_list = jax.random.split(jax.random.key(seed), 15)
    return {
        "lengths": uneven(key_list[0], NDOC, SEQUENCE_LENGTH, DOC_MOST, 2).astype(jnp.int32),
        "queries": draw_queries(jax.random.fold_in(key_list[14], 71), 0),
        "keys": draw_keys(jax.random.fold_in(key_list[14], 71), 0),
        "values": gaussian(key_list[3], (SEQUENCE_LENGTH, KEY_VALUE_HEADS * HEAD_SIZE), 1.0, 6.0, ((0, 32), (1, 8))),
        "ssm_input": gaussian(key_list[4], (SEQUENCE_LENGTH, SH * SP), 1.0, 6.0, ((0, 32), (1, 8))),
        "gate_input": gaussian(key_list[5], (SEQUENCE_LENGTH, SH * SP), 1.0, 6.0, ((0, 32), (1, 8))),
        "b_input": gaussian(key_list[6], (SEQUENCE_LENGTH, G * SN), (SN ** -0.5), 1.25, ((0, 32), (1, 8))),
        "c_input": gaussian(key_list[7], (SEQUENCE_LENGTH, G * SN), 1.0, 6.0, ((0, 32), (1, 8))),
        "log_decay": draw_log_decay(jax.random.fold_in(key_list[14], 71), 0),
        "skip": jnp.clip(jnp.exp(math.log(2.0) - 1.3862944 * jax.random.uniform(key_list[9], (SH,), jnp.float32) ** shard_levels(key_list[9], (SH,), ((0, 8),), -0.2, 0.2)), 0.5, 2.0),
        "norm_gain": jnp.clip(1.0 + 0.1 * jax.random.normal(key_list[10], (SH * SP,), jnp.float32), 0.5, 1.5),
        "attn_out_weight": gaussian(key_list[11], (QH * HEAD_SIZE, D), (QH * HEAD_SIZE) ** -0.5, 0.125, ((0, 8),)),
        "ssm_out_weight": gaussian(key_list[12], (SH * SP, D), (SH * SP) ** -0.5, 0.09375, ((0, 8),)),
        "cotangent": bell_draw_with(key_list[13], (SEQUENCE_LENGTH, D), 1.0, 6.0, ((0, 32), (1, 8)), (0, 1, 32, 2.75)),
    }


def doc_info(lengths, positions):
    ends = jnp.cumsum(lengths).astype(jnp.int32)
    begins = (ends - lengths).astype(jnp.int32)
    docs = lax.optimization_barrier(jnp.sum((positions[:, None] >= ends[None, :]).astype(jnp.int32), axis=1)).astype(jnp.int32)
    starts = jnp.any(positions[:, None] == begins[None, :], axis=1)
    return (docs, starts)

def attend(carry, queries, qpos, qdoc, keys, values, key_position, kdoc):
    m_old, l_old, accum = carry
    scores = jnp.einsum('tkgd,nkd->kgtn', queries.astype(jnp.float32), keys.astype(jnp.float32)) * HEAD_SIZE ** (-0.5)
    allowed = (kdoc[None, :] == qdoc[:, None]) & (key_position[None, :] <= qpos[:, None]) & (key_position[None, :] >= 0)
    m_blk = lax.optimization_barrier(jnp.max(jnp.where(allowed, scores, -1e+30), axis=-1))
    m_new = jnp.maximum(m_old, m_blk)
    probs = jnp.where(allowed, jnp.exp(scores - m_new[..., None]), 0.0)
    factor = jnp.exp(m_old - m_new)
    l_new = l_old * factor + lax.optimization_barrier(jnp.sum(probs, axis=-1))
    weights = probs.astype(jnp.bfloat16)
    accum = accum * factor[..., None] + jnp.einsum('kgtn,nkd->kgtd', weights.astype(jnp.float32), values.astype(jnp.float32))
    return (m_new, l_new, accum)

def attend_block(carry, queries, qpos, qdoc, keys, values, key_position, kdoc):
    useful = (kdoc[-1] >= qdoc[0]) & (kdoc[0] <= qdoc[-1]) & (key_position[0] <= qpos[-1]) & (key_position[-1] >= 0)

    def update(state):
        return attend(state, queries, qpos, qdoc, keys, values, key_position, kdoc)

    def unchanged(state):
        return state
    return lax.cond(useful, update, unchanged, carry)

def attention_all(queries, keys, values, lengths):
    grp = QH // KEY_VALUE_HEADS
    visit_order = jnp.arange(TOKENS_PER_PARTITION, dtype=jnp.int32)

    def one_block(block_number):
        leading_block = (block_number * TOKENS_PER_PARTITION).astype(jnp.int32)
        qblock = lax.dynamic_slice_in_dim(queries, leading_block, TOKENS_PER_PARTITION, 0).reshape(TOKENS_PER_PARTITION, KEY_VALUE_HEADS, grp, HEAD_SIZE)
        qpos = (leading_block + visit_order).astype(jnp.int32)
        qdoc, _ = doc_info(lengths, qpos)

        def visit(backward_step, state):
            key_index = (block_number - backward_step).astype(jnp.int32)
            key_start = (jnp.maximum(key_index, 0) * TOKENS_PER_PARTITION).astype(jnp.int32)
            key_position = (key_index * TOKENS_PER_PARTITION + visit_order).astype(jnp.int32)
            kdoc, _ = doc_info(lengths, key_position)
            kblock = lax.dynamic_slice_in_dim(keys, key_start, TOKENS_PER_PARTITION, 0).reshape(TOKENS_PER_PARTITION, KEY_VALUE_HEADS, HEAD_SIZE)
            vblock = lax.dynamic_slice_in_dim(values, key_start, TOKENS_PER_PARTITION, 0).reshape(TOKENS_PER_PARTITION, KEY_VALUE_HEADS, HEAD_SIZE)
            return attend_block(state, qblock, qpos, qdoc, kblock, vblock, key_position, kdoc)
        start = (jnp.full((KEY_VALUE_HEADS, grp, TOKENS_PER_PARTITION), -1e+30, jnp.float32), jnp.zeros((KEY_VALUE_HEADS, grp, TOKENS_PER_PARTITION), jnp.float32), jnp.zeros((KEY_VALUE_HEADS, grp, TOKENS_PER_PARTITION, HEAD_SIZE), jnp.float32))
        m_fin, l_fin, accum = lax.fori_loop(jnp.int32(0), jnp.int32(VISIBLE_BLOCKS + 1), visit, start)
        normalized = accum / l_fin[..., None]
        return normalized.transpose(2, 0, 1, 3).reshape(TOKENS_PER_PARTITION, QH * HEAD_SIZE).astype(jnp.bfloat16)
    return lax.map(one_block, jnp.arange(N_CTX, dtype=jnp.int32)).reshape(SEQUENCE_LENGTH, QH * HEAD_SIZE)

def ssm_block(inputs, b_in, c_in, log_decay, positions, lengths):
    rows = inputs.shape[0]
    heads = log_decay.shape[1]
    groups = b_in.shape[1] // SN
    per = heads // groups
    xh = inputs.reshape(rows, groups, per, SP)
    bg = b_in.reshape(rows, groups, SN).astype(jnp.float32)
    cg = c_in.reshape(rows, groups, SN).astype(jnp.float32)
    docs, starts = doc_info(lengths, positions)
    cum = jnp.cumsum(log_decay, axis=0)
    visit_order = jnp.arange(rows, dtype=jnp.int32)
    same = (docs[:, None] == docs[None, :]) & (visit_order[None, :] <= visit_order[:, None])
    diff = cum.T[:, :, None] - cum.T[:, None, :]
    decay = jnp.where(same[None], jnp.exp(jnp.where(same[None], diff, 0.0)), 0.0)
    inner = jnp.einsum('tgn,sgn->gts', cg, bg)
    mixing = (decay.reshape(groups, per, rows, rows) * inner[:, None]).astype(jnp.bfloat16)
    y_inner = jnp.einsum('ghts,sghp->tghp', mixing.astype(jnp.float32), xh.astype(jnp.float32))
    alive = jnp.cumsum(starts.astype(jnp.int32)) == 0
    total = jnp.where(alive[-1], jnp.exp(cum[-1]), 0.0)
    tail = jnp.where((docs == docs[-1])[:, None], jnp.exp(cum[-1][None, :] - cum), 0.0)
    scaled = (tail[:, :, None] * inputs.reshape(rows, heads, SP).astype(jnp.float32)).reshape(rows, groups, per, SP)
    local = jnp.einsum('tgn,tghp->ghnp', bg, scaled, precision=lax.Precision.HIGHEST).reshape(heads, SN, SP)
    reach_in = jnp.where(alive[:, None], jnp.exp(cum), 0.0)
    return (y_inner, total, local, cg, reach_in)

def ssm_finish(y_inner, cg, reach_in, state_in, inputs, gates, skip, norm_gain):
    rows, groups, per, _ = y_inner.shape
    y_carry = jnp.einsum('tgn,ghnp->tghp', cg, state_in.reshape(groups, per, SN, SP), precision=lax.Precision.HIGHEST)
    y_carry = y_carry * reach_in.reshape(rows, groups, per)[..., None]
    xh = inputs.reshape(rows, groups, per, SP).astype(jnp.float32)
    y_all = y_inner + y_carry + skip.reshape(groups, per)[None, :, :, None] * xh
    gated = y_all * jax.nn.silu(gates.reshape(rows, groups, per, SP).astype(jnp.float32))
    flat = gated.reshape(rows, groups, per * SP)
    normed = flat * lax.rsqrt(lax.optimization_barrier(jnp.mean(flat * flat, axis=-1, keepdims=True)) + 1e-05)
    return (normed.reshape(rows, groups * per * SP) * norm_gain).astype(jnp.bfloat16)

def ssm_all(ssm_input, gate_input, b_input, c_input, log_decay, skip, norm_gain, lengths):
    visit_order = jnp.arange(TOKENS_PER_PARTITION, dtype=jnp.int32)

    def step(state, item):
        inputs, gates, b_in, c_in, decays, block_number = item
        positions = (block_number * TOKENS_PER_PARTITION + visit_order).astype(jnp.int32)
        y_inner, total, local, cg, reach_in = ssm_block(inputs, b_in, c_in, decays, positions, lengths)
        out = ssm_finish(y_inner, cg, reach_in, state, inputs, gates, skip, norm_gain)
        return (total[:, None, None] * state + local, out)
    items = (ssm_input.reshape(N_CTX, TOKENS_PER_PARTITION, SH * SP), gate_input.reshape(N_CTX, TOKENS_PER_PARTITION, SH * SP), b_input.reshape(N_CTX, TOKENS_PER_PARTITION, G * SN), c_input.reshape(N_CTX, TOKENS_PER_PARTITION, G * SN), log_decay.reshape(N_CTX, TOKENS_PER_PARTITION, SH), jnp.arange(N_CTX, dtype=jnp.int32))
    _, outs = lax.scan(step, jnp.zeros((SH, SN, SP), jnp.float32), items)
    return outs.reshape(SEQUENCE_LENGTH, SH * SP)

def reference(lengths, queries, keys, values, ssm_input, gate_input, b_input, c_input, log_decay, skip, norm_gain, attn_out_weight, ssm_out_weight, cotangent):
    attn_out = attention_all(queries, keys, values, lengths)
    ssm_out = ssm_all(ssm_input, gate_input, b_input, c_input, log_decay, skip, norm_gain, lengths)
    attn_part = QH * HEAD_SIZE // N_TP
    ssm_part = SH * SP // N_TP

    def step(grads, item):
        attn_block, ssm_block_out, cot_block = item
        mixed = jnp.zeros((TOKENS_PER_PARTITION, D), jnp.float32)
        for part in range(N_TP):
            term = jnp.dot(attn_block[:, part * attn_part:(part + 1) * attn_part], attn_out_weight[part * attn_part:(part + 1) * attn_part], preferred_element_type=jnp.float32)
            term = term + jnp.dot(ssm_block_out[:, part * ssm_part:(part + 1) * ssm_part], ssm_out_weight[part * ssm_part:(part + 1) * ssm_part], preferred_element_type=jnp.float32)
            mixed = mixed + lax.optimization_barrier(term.astype(jnp.bfloat16)).astype(jnp.float32)
        joined = jnp.concatenate([attn_block, ssm_block_out], axis=1)
        term = lax.dot_general(cot_block, joined, (((0,), (0,)), ((), ())), preferred_element_type=jnp.float32)
        grads = grads + lax.optimization_barrier(term.astype(jnp.bfloat16)).astype(jnp.float32)
        return (grads, mixed.astype(jnp.bfloat16))
    items = (attn_out.reshape(N_CTX, TOKENS_PER_PARTITION, QH * HEAD_SIZE), ssm_out.reshape(N_CTX, TOKENS_PER_PARTITION, SH * SP), cotangent.reshape(N_CTX, TOKENS_PER_PARTITION, D))
    grads, mixed = lax.scan(step, jnp.zeros((D, HID), jnp.float32), items)
    return (mixed.reshape(SEQUENCE_LENGTH, D), grads[:, :QH * HEAD_SIZE], grads[:, QH * HEAD_SIZE:])
```

```python
import functools

import jax
import jax.numpy as jnp
from jax import lax
from jax.experimental import pallas as pl
from jax.experimental.pallas import tpu as pltpu
from jax.sharding import Mesh
from jax.sharding import PartitionSpec as P

HEAD = 128
GRP = 2
SP = 64
SN = 128
NY = 4
NZ = 8
NX = 4
NC = 2
YZ = ("y", "z")
F32 = jnp.float32
BF = jnp.bfloat16
HI = lax.Precision.HIGHEST
LOW = -1e30
LIMIT = 48 * 1024 * 1024


def shift(value, axis, steps, cyclic=True):
    n = lax.axis_size(axis)
    pairs = [(i, (i + steps) % n) for i in range(n) if cyclic or 0 <= i + steps < n]
    return lax.ppermute(value, axis, pairs)


def call(kernel, outs, cost=None, **kw):
    return pl.pallas_call(
        kernel,
        out_shape=outs,
        compiler_params=pltpu.CompilerParams(vmem_limit_bytes=LIMIT),
        cost_estimate=cost,
        **kw,
    )


def cost(flops, nbytes, exps=0):
    return pl.CostEstimate(flops=int(flops), bytes_accessed=int(nbytes), transcendentals=int(exps))


def mm(a, b, dims=((1,), (0,)), precision=None):
    return lax.dot_general(a, b, (dims, ((), ())), preferred_element_type=F32, precision=precision)


def spread(pairs, lane):
    return jnp.where(lane < SP, pairs[0], pairs[1])


def ssm_first(x_ref, b_ref, c_ref, ld_ref, first_ref, skip_ref, y_ref, state_ref, cum_ref):
    rows = x_ref.shape[0]
    row = lax.broadcasted_iota(jnp.int32, (rows, rows), 0)
    col = lax.broadcasted_iota(jnp.int32, (rows, rows), 1)
    lower = jnp.where(col <= row, 1.0, 0.0).astype(F32)
    cum = mm(lower, ld_ref[...], precision=HI)
    cum_ref[...] = cum
    cum_t = cum.T
    first = first_ref[...]
    mask = (col <= row) & (col >= first)
    inner = mm(c_ref[...], b_ref[...], ((1,), (1,)))
    last = cum[rows - 1 : rows, :]
    last_first = first[rows - 1 : rows, :]
    r1 = lax.broadcasted_iota(jnp.int32, (rows, 1), 0)
    tail = jnp.where(r1 >= last_first, jnp.exp(last - cum), 0.0)
    lane = lax.broadcasted_iota(jnp.int32, (rows, 2 * SP), 1)
    b_t = b_ref[...].astype(F32).T.astype(BF)
    for p in range(4):
        x = x_ref[:, p * 128 : (p + 1) * 128]
        y = []
        for h in (2 * p, 2 * p + 1):
            diff = jnp.where(mask, cum[:, h : h + 1] - cum_t[h : h + 1, :], LOW)
            mixing = (jnp.exp(diff) * inner).astype(BF)
            y.append(mm(mixing, x))
        xf = x.astype(F32)
        y_ref[:, p * 128 : (p + 1) * 128] = spread(y, lane) + skip_ref[:, p * 128 : (p + 1) * 128] * xf
        scaled = spread([tail[:, 2 * p : 2 * p + 1], tail[:, 2 * p + 1 : 2 * p + 2]], lane) * xf
        state_ref[:, p * 128 : (p + 1) * 128] = mm(b_t, scaled.astype(BF)).astype(BF)
    total = jnp.where(last_first < 0, jnp.exp(last), 0.0)
    high = total.astype(BF).astype(F32)
    r2 = lax.broadcasted_iota(jnp.int32, (SN, 128), 0)
    state_ref[:, 512:] = jnp.where(r2 % 16 < 8, high, total - high).astype(BF)


def heads_matrix():
    h = lax.broadcasted_iota(jnp.int32, (128, 512), 0)
    l = lax.broadcasted_iota(jnp.int32, (128, 512), 1)
    return jnp.where((l >= h * SP) & (l < (h + 1) * SP), 1.0, 0.0).astype(F32)


def unpack_total(block):
    side = block[:, 512:].astype(F32)
    return side[0:1, :] + side[8:9, :]


def ssm_scan(g_ref, e_ref, p_ref, r_ref):
    totals = jnp.concatenate([unpack_total(g_ref[i]) for i in range(NZ)], axis=0)
    wide = mm(totals, heads_matrix(), precision=HI)
    acc = jnp.zeros((16, 512), F32)
    prod = jnp.ones((1, 512), F32)
    small = jnp.ones((1, 128), F32)
    for i in range(NZ):
        e_ref[i] = acc
        p_ref[i : i + 1, :] = prod
        t = wide[i : i + 1, :]
        acc = t * acc + g_ref[i][:, :512].astype(F32)
        prod = prod * t
        small = small * totals[i : i + 1, :]
    r_ref[:, :512] = acc.astype(BF)
    high = small.astype(BF).astype(F32)
    r2 = lax.broadcasted_iota(jnp.int32, (16, 128), 0)
    r_ref[:, 512:] = jnp.where(r2 < 8, high, small - high).astype(BF)


def ssm_join(e_ref, p_ref, one_ref, two_ref, out_ref):
    one, two = one_ref[...], two_ref[...]
    total = jnp.broadcast_to(unpack_total(one), (8, 128))
    wide = mm(total, heads_matrix(), precision=HI)[0:1, :]
    carry = one[:, :512].astype(F32) + wide * two[:, :512].astype(F32)
    for i in range(NZ):
        out_ref[i] = (e_ref[i] + p_ref[i : i + 1, :] * carry).astype(BF)


def ssm_last(c_ref, state_ref, y_ref, cum_ref, first_ref, gate_ref, gain_ref, out_ref):
    rows = c_ref.shape[0]
    reach = jnp.where(first_ref[...] < 0, jnp.exp(cum_ref[...]), 0.0)
    lane = lax.broadcasted_iota(jnp.int32, (rows, 2 * SP), 1)
    gated = []
    squares = jnp.zeros((rows, 1), F32)
    for p in range(4):
        cols = slice(p * 128, (p + 1) * 128)
        carried = mm(c_ref[...], state_ref[:, cols])
        carried = carried * spread([reach[:, 2 * p : 2 * p + 1], reach[:, 2 * p + 1 : 2 * p + 2]], lane)
        gate = gate_ref[:, cols].astype(F32)
        u = (y_ref[:, cols] + carried) * (gate / (1.0 + jnp.exp(-gate)))
        squares = squares + jnp.sum(u * u, axis=1, keepdims=True)
        gated.append(u)
    scale = lax.rsqrt(squares / 512.0 + 1e-05)
    for p in range(4):
        cols = slice(p * 128, (p + 1) * 128)
        out_ref[:, cols] = (gated[p] * scale * gain_ref[:, cols]).astype(BF)


def attn_kernel(offsets, first, last, *refs):
    q_ref, start_ref, *rest = refs
    n = len(offsets)
    blocks, rest = rest[: (n + 1) // 2 if n > 1 else 1], rest[(n + 1) // 2 if n > 1 else 1 :]
    if not first:
        m_in, l_in, a_in, *rest = rest
    rows = q_ref.shape[0]
    q = jnp.concatenate([q_ref[:, :HEAD], q_ref[:, HEAD:]], axis=0)
    start = start_ref[...]
    start = jnp.concatenate([start, start], axis=0)
    col = lax.broadcasted_iota(jnp.int32, (2 * rows, rows), 1)
    scores, values = [], []
    for i, offset in enumerate(offsets):
        ref = blocks[i // 2]
        at = (i % 2) * 2 * HEAD
        s = mm(q, ref[:, at : at + HEAD], ((1,), (1,))) * HEAD**-0.5
        allowed = col + offset * rows >= start
        if offset == 0:
            row = lax.broadcasted_iota(jnp.int32, (rows, rows), 0)
            row = jnp.concatenate([row, row], axis=0)
            allowed = allowed & (col <= row)
        scores.append(jnp.where(allowed, s, LOW))
        values.append(ref[:, at + HEAD : at + 2 * HEAD])
    top = scores[0]
    for s in scores[1:]:
        top = jnp.maximum(top, s)
    m = jnp.max(top, axis=1, keepdims=True)
    if not first:
        m_old = m_in[:, 0:1]
        m = jnp.maximum(m, m_old)
    l, a = None, None
    for s, v in zip(scores, values):
        p = jnp.exp(s - m)
        row_sum = jnp.sum(p, axis=1, keepdims=True)
        part = mm(p.astype(BF), v)
        l = row_sum if l is None else l + row_sum
        a = part if a is None else a + part
    if not first:
        factor = jnp.exp(m_old - m)
        l = l + l_in[:, 0:1] * factor
        a = a + a_in[...] * factor
    if last:
        (out_ref,) = rest
        o = (a / l).astype(BF)
        out_ref[:, :HEAD] = o[:rows]
        out_ref[:, HEAD:] = o[rows:]
    else:
        m_ref, l_ref, a_ref = rest
        m_ref[...] = jnp.broadcast_to(m, m_ref.shape)
        l_ref[...] = jnp.broadcast_to(l, l_ref.shape)
        a_ref[...] = a


def attend(q, start, blocks, offsets, state, last):
    rows = q.shape[0]
    carry = jax.ShapeDtypeStruct((2 * rows, HEAD), F32)
    outs = jax.ShapeDtypeStruct((rows, 2 * HEAD), BF) if last else (carry,) * 3
    n = len(offsets)
    kernel = functools.partial(attn_kernel, offsets, state is None, last)
    c = cost(n * 4 * 2 * rows * rows * HEAD, 2**20, n * 2 * rows * rows)
    return call(kernel, outs, c)(q, start, *blocks, *(state or ()))


def project_kernel(which_ref, a_ref, s_ref, wa_ref, ws_ref, o_ref):
    o_ref[...] = (mm(a_ref[...], wa_ref[...]) + mm(s_ref[...], ws_ref[...])).astype(BF)


def project(which, attn, ssm, wa, ws):
    rows, width = attn.shape[0], wa.shape[1] // (NX * NC)
    grid = pltpu.PrefetchScalarGridSpec(
        num_scalar_prefetch=1,
        grid=(NX,),
        in_specs=[
            pl.BlockSpec(attn.shape, lambda j, w: (0, 0)),
            pl.BlockSpec(ssm.shape, lambda j, w: (0, 0)),
            pl.BlockSpec((wa.shape[0], width), lambda j, w: (0, NC * j + w[0])),
            pl.BlockSpec((ws.shape[0], width), lambda j, w: (0, NC * j + w[0])),
        ],
        out_specs=pl.BlockSpec((rows, width), lambda j, w: (0, j)),
    )
    k = attn.shape[1] + ssm.shape[1]
    c = cost(2 * rows * k * NX * width, 2 * k * NX * width)
    return call(project_kernel, jax.ShapeDtypeStruct((rows, NX * width), BF), c, grid_spec=grid)(
        which, attn, ssm, wa, ws
    )


def gather_y(value):
    return jnp.concatenate([value] + [shift(value, "y", k) for k in range(1, NY)], axis=0)


def add(a, b):
    return (a.astype(F32) + b.astype(F32)).astype(BF)


def scatter_z(terms):
    size = terms.shape[0] // NZ
    piece = lambda d: terms[(d % NZ) * size : (d % NZ + 1) * size]
    right, left = piece(4), piece(-3)
    for k in range(4):
        new_right = shift(right, "z", 1)
        if k < 3:
            new_left = shift(left, "z", -1)
            left = add(new_left, piece(k - 2)) if k < 2 else new_left
        right = add(new_right, piece(3 - k)) if k < 3 else new_right
    return right.astype(F32) + left.astype(F32) + piece(0).astype(F32)


def body(
    lengths,
    queries,
    keys,
    values,
    ssm_input,
    gate_input,
    b_input,
    c_input,
    log_decay,
    skip,
    norm_gain,
    attn_out_weight,
    ssm_out_weight,
    cotangent,
):
    rows = queries.shape[0]
    x, c, y, z = (lax.axis_index(a) for a in ("x", "c", "y", "z"))
    base = (y * NZ + z) * rows
    begins = jnp.cumsum(lengths) - lengths
    position = base + jnp.arange(rows, dtype=jnp.int32)
    begin = jnp.max(jnp.where(begins[None, :] <= position[:, None], begins[None, :], 0), axis=1)
    first = (begin - base).astype(jnp.int32)[:, None]

    kv = jnp.concatenate([keys, values], axis=1)
    far8, far16 = shift(kv, YZ, 8, False), shift(kv, YZ, 16, False)
    right = jnp.concatenate([kv, far8], axis=1)
    left = jnp.concatenate([far8, far16], axis=1)

    decays = jnp.pad(log_decay, ((0, 0), (0, 128 - log_decay.shape[1])))
    wide_skip = jnp.repeat(skip, SP)[None, :]
    y_local, packed, cum = call(
        ssm_first,
        (
            jax.ShapeDtypeStruct((rows, 512), F32),
            jax.ShapeDtypeStruct((SN, 640), BF),
            jax.ShapeDtypeStruct((rows, 128), F32),
        ),
        cost(2 * rows * rows * 128 * 10, 2**21, 8 * rows * rows),
    )(ssm_input, b_input, c_input, decays, first, wide_skip)
    slices = lax.all_to_all(packed.reshape(NZ, 16, 640), "z", 0, 0)
    inside, products, row_total = call(
        ssm_scan,
        (
            jax.ShapeDtypeStruct((NZ, 16, 512), F32),
            jax.ShapeDtypeStruct((NZ, 512), F32),
            jax.ShapeDtypeStruct((16, 640), BF),
        ),
    )(slices)
    one, two = shift(row_total, "y", 1, False), shift(row_total, "y", 2, False)
    joined = call(ssm_join, jax.ShapeDtypeStruct((NZ, 16, 512), BF))(inside, products, one, two)
    state_in = lax.all_to_all(joined, "z", 0, 0).reshape(SN, 512)
    ssm_out = call(
        ssm_last,
        jax.ShapeDtypeStruct((rows, 512), BF),
        cost(2 * rows * 128 * 512, 2**20, rows * 512),
    )(c_input, state_in, y_local, cum, first, gate_input, norm_gain[None, :])

    att = attend(queries, first, [kv], [0], None, False)
    att = attend(queries, first, [left], [-8, -16], att, False)
    for k in range(1, 5):
        right = shift(right, YZ, 1, False)
        blocks, offsets = [right], [-k, -8 - k]
        if k < 4:
            left = shift(left, YZ, -1, False)
            blocks, offsets = blocks + [left], offsets + [k - 8, k - 16]
        att = attend(queries, first, blocks, offsets, att, k == 4)
    attn_out = att

    cots = jnp.stack([cotangent] + [shift(cotangent, "x", k) for k in range(1, NX)])
    slab = lambda k: lax.dynamic_index_in_dim(cots, (x - y - k) % NX, 0, False)
    mine = jnp.concatenate([slab(0)] + [shift(slab(k), "y", k) for k in range(1, NY)], axis=0)
    other = shift(mine, "c", 1)
    full = jnp.concatenate([jnp.where(c == 0, mine, other), jnp.where(c == 0, other, mine)], axis=1).T
    size = full.shape[0] // NZ
    cot_t = lax.dynamic_slice_in_dim(jnp.concatenate([full, full], axis=0), z * size, NZ * size, 0)

    def grads(out):
        return scatter_z(jnp.dot(cot_t, gather_y(out), preferred_element_type=F32).astype(BF))

    grad_ssm = grads(ssm_out)
    grad_attn = grads(attn_out)

    core = jnp.full((1,), c, jnp.int32)
    give = project(1 - core, attn_out, ssm_out, attn_out_weight, ssm_out_weight)
    keep = project(core, attn_out, ssm_out, attn_out_weight, ssm_out_weight)
    pair = add(keep, shift(give, "c", 1))
    width = cotangent.shape[1]
    part = lambda k: lax.dynamic_slice_in_dim(pair, ((x + k) % NX) * width, width, 1)
    mixed = part(0).astype(F32)
    for k in range(1, NX):
        mixed = mixed + shift(part(k), "x", k).astype(F32)
    return mixed.astype(BF), grad_attn, grad_ssm


def solution(mesh):
    fine = Mesh(mesh.devices.reshape(NY, NZ, NX, NC), ("y", "z", "x", "c"))
    tp = ("x", "c")
    both = P(YZ, tp)
    placed = (P(),) + (both,) * 8 + (P(tp), P(tp), P(tp, None), P(tp, None), both)
    return jax.shard_map(
        body, mesh=fine, in_specs=placed, out_specs=(both, both, both), check_vma=False
    )
```

```python
import functools

import jax
import jax.numpy as jnp
from jax import lax
from jax.experimental import pallas as pl
from jax.experimental.pallas import tpu as pltpu
from jax.sharding import Mesh
from jax.sharding import PartitionSpec as P

HEAD = 128
GRP = 2
SP = 64
SN = 128
NY = 4
NZ = 8
NX = 4
NC = 2
YZ = ("y", "z")
F32 = jnp.float32
BF = jnp.bfloat16
HI = lax.Precision.HIGHEST
LOW = -1e30
LOG2E = 1.4426950408889634
SPLIT = 2
LIMIT = 16 * 1024 * 1024
WIDE = 54 * 1024 * 1024


def shift(value, axis, steps, cyclic=True):
    n = lax.axis_size(axis)
    pairs = [(i, (i + steps) % n) for i in range(n) if cyclic or 0 <= i + steps < n]
    return lax.ppermute(value, axis, pairs)


def call(kernel, outs, cost=None, limit=LIMIT, **kw):
    return pl.pallas_call(
        kernel,
        out_shape=outs,
        compiler_params=pltpu.CompilerParams(vmem_limit_bytes=limit),
        cost_estimate=cost,
        **kw,
    )


def cost(flops, nbytes, exps=0):
    return pl.CostEstimate(flops=int(flops), bytes_accessed=int(nbytes), transcendentals=int(exps))


def mm(a, b, dims=((1,), (0,)), precision=None):
    return lax.dot_general(a, b, (dims, ((), ())), preferred_element_type=F32, precision=precision)


def spread(pairs, lane):
    return jnp.where(lane < SP, pairs[0], pairs[1])


def ssm_first(
    base_ref, len_hbm, x_hbm, b_hbm, c_hbm, ld_hbm, skip_hbm, y_ref, state_ref, cum_ref, first_ref,
    len_ref, x_ref, b_ref, c_ref, ld_ref, skip_ref, sems,
):
    pairs = [(ld_hbm, ld_ref), (len_hbm, len_ref), (b_hbm, b_ref), (c_hbm, c_ref), (x_hbm, x_ref), (skip_hbm, skip_ref)]
    copies = [pltpu.make_async_copy(src, dst, sems.at[i]) for i, (src, dst) in enumerate(pairs)]
    for copy in copies:
        copy.start()
    for copy in copies:
        copy.wait()
    rows = x_ref.shape[0]
    r1 = lax.broadcasted_iota(jnp.int32, (rows, 1), 0)
    base = base_ref[0]
    begin, first = jnp.int32(0), jnp.zeros((rows, 1), jnp.int32) - base
    for j in range(len_ref.shape[0]):
        first = jnp.where(r1 + base >= begin, begin - base, first)
        begin = begin + len_ref[j]
    first_ref[...] = first
    row = lax.broadcasted_iota(jnp.int32, (rows, rows), 0)
    col = lax.broadcasted_iota(jnp.int32, (rows, rows), 1)
    lower = jnp.where(col <= row, 1.0, 0.0).astype(F32)
    heads = ld_ref.shape[0]
    l = lax.broadcasted_iota(jnp.int32, (128, heads), 0)
    h = lax.broadcasted_iota(jnp.int32, (128, heads), 1)
    decays = mm(jnp.where(h == l, 1.0, 0.0).astype(F32), ld_ref[...], precision=HI)
    cum = mm(lower, decays, ((1,), (1,)), precision=HI)
    cum_ref[...] = cum
    cum_t = cum.T
    mask = (col <= row) & (col >= first)
    inner = mm(c_ref[...], b_ref[...], ((1,), (1,)))
    last = cum[rows - 1 : rows, :]
    last_first = first[rows - 1 : rows, :]
    tail = jnp.where(r1 >= last_first, jnp.exp(last - cum), 0.0)
    lane = lax.broadcasted_iota(jnp.int32, (rows, 2 * SP), 1)
    b_t = b_ref[...].astype(F32).T.astype(BF)
    skip = mm(skip_ref[...], heads_matrix(heads), precision=HI)
    for p in range(4):
        x = x_ref[:, p * 128 : (p + 1) * 128]
        y = []
        for h in (2 * p, 2 * p + 1):
            diff = jnp.where(mask, cum[:, h : h + 1] - cum_t[h : h + 1, :], LOW)
            mixing = (jnp.exp(diff) * inner).astype(BF)
            y.append(mm(mixing, x))
        xf = x.astype(F32)
        y_ref[:, p * 128 : (p + 1) * 128] = spread(y, lane) + skip[:, p * 128 : (p + 1) * 128] * xf
        scaled = spread([tail[:, 2 * p : 2 * p + 1], tail[:, 2 * p + 1 : 2 * p + 2]], lane) * xf
        state_ref[:, p * 128 : (p + 1) * 128] = mm(b_t, scaled.astype(BF)).astype(BF)
    total = jnp.where(last_first < 0, jnp.exp(last), 0.0)
    high = total.astype(BF).astype(F32)
    r2 = lax.broadcasted_iota(jnp.int32, (SN, 128), 0)
    state_ref[:, 512:] = jnp.where(r2 % 16 < 8, high, total - high).astype(BF)


def heads_matrix(n=128):
    h = lax.broadcasted_iota(jnp.int32, (n, 512), 0)
    l = lax.broadcasted_iota(jnp.int32, (n, 512), 1)
    return jnp.where((l >= h * SP) & (l < (h + 1) * SP), 1.0, 0.0).astype(F32)


def unpack_total(block):
    side = block[:, 512:].astype(F32)
    return side[0:1, :] + side[8:9, :]


def ssm_scan(g_ref, e_ref, p_ref, r_ref):
    totals = jnp.concatenate([unpack_total(g_ref[i]) for i in range(NZ)], axis=0)
    wide = mm(totals, heads_matrix(), precision=HI)
    acc = jnp.zeros((16, 512), F32)
    prod = jnp.ones((1, 512), F32)
    small = jnp.ones((1, 128), F32)
    for i in range(NZ):
        e_ref[i] = acc
        p_ref[i : i + 1, :] = prod
        t = wide[i : i + 1, :]
        acc = t * acc + g_ref[i][:, :512].astype(F32)
        prod = prod * t
        small = small * totals[i : i + 1, :]
    r_ref[:, :512] = acc.astype(BF)
    high = small.astype(BF).astype(F32)
    r2 = lax.broadcasted_iota(jnp.int32, (16, 128), 0)
    r_ref[:, 512:] = jnp.where(r2 < 8, high, small - high).astype(BF)


def ssm_join(e_ref, p_ref, one_ref, two_ref, out_ref):
    one, two = one_ref[...], two_ref[...]
    total = jnp.broadcast_to(unpack_total(one), (8, 128))
    wide = mm(total, heads_matrix(), precision=HI)[0:1, :]
    carry = one[:, :512].astype(F32) + wide * two[:, :512].astype(F32)
    for i in range(NZ):
        out_ref[i] = (e_ref[i] + p_ref[i : i + 1, :] * carry).astype(BF)


def ssm_last(c_ref, state_ref, y_ref, cum_ref, first_ref, gate_ref, gain_ref, out_ref):
    rows = c_ref.shape[0]
    reach = jnp.where(first_ref[...] < 0, jnp.exp(cum_ref[...]), 0.0)
    lane = lax.broadcasted_iota(jnp.int32, (rows, 2 * SP), 1)
    gated = []
    squares = jnp.zeros((rows, 1), F32)
    for p in range(4):
        cols = slice(p * 128, (p + 1) * 128)
        carried = mm(c_ref[...], state_ref[:, cols])
        carried = carried * spread([reach[:, 2 * p : 2 * p + 1], reach[:, 2 * p + 1 : 2 * p + 2]], lane)
        gate = gate_ref[:, cols].astype(F32)
        u = (y_ref[:, cols] + carried) * (gate / (1.0 + jnp.exp(-gate)))
        squares = squares + jnp.sum(u * u, axis=1, keepdims=True)
        gated.append(u)
    scale = lax.rsqrt(squares / 512.0 + 1e-05)
    for p in range(4):
        cols = slice(p * 128, (p + 1) * 128)
        out_ref[:, cols] = (gated[p] * scale * gain_ref[:, cols]).astype(BF)


def pick_kernel(at_ref, *refs):
    for k in range(NY):
        for j in range(NX):

            @pl.when(at_ref[k] == j)
            def _():
                refs[NX + k][...] = refs[j][...]


def merge(q, start, blocks, carry, rows, causal_first=False):
    col = lax.broadcasted_iota(jnp.int32, (2 * rows, rows), 1)
    scores = []
    for i, (key, _, offset) in enumerate(blocks):
        s = mm(q, key, ((1,), (1,))) * (HEAD**-0.5 * LOG2E)
        allowed = col >= start - offset
        if causal_first and i == 0:
            row = lax.broadcasted_iota(jnp.int32, (rows, rows), 0)
            allowed = allowed & (col <= jnp.concatenate([row, row], axis=0))
        scores.append(jnp.where(allowed, s, LOW))
    top = functools.reduce(jnp.maximum, scores)
    m = jnp.max(top, axis=1, keepdims=True)
    if carry is not None:
        m = jnp.maximum(m, carry[0])
    p = [jnp.exp2(s - m) for s in scores]
    l = jnp.sum(functools.reduce(jnp.add, p), axis=1, keepdims=True)
    a = functools.reduce(jnp.add, [mm(w.astype(BF), v) for w, (_, v, _) in zip(p, blocks)])
    if carry is not None:
        factor = jnp.exp2(carry[0] - m)
        l, a = l + carry[1] * factor, a + carry[2] * factor
    return m, l, a


def heads_below(q_ref, first_ref):
    q = jnp.concatenate([q_ref[:, :HEAD], q_ref[:, HEAD:]], axis=0)
    start = first_ref[...]
    return q, jnp.concatenate([start, start], axis=0)


def attn_kernel(z_ref, kv_hbm, q_ref, first_ref, out_ref, kv_ref, sems):
    rows = q_ref.shape[0]
    z = z_ref[0]
    sources = [kv_hbm.at[z, pl.ds(0, rows)]]
    offsets = [jnp.int32(0)]
    for j in range(NZ):
        later = j >= z
        at = pl.multiple_of(jnp.where(later, 2 * rows, 0), rows)
        sources += [kv_hbm.at[j, pl.ds(rows, rows)], kv_hbm.at[j, pl.ds(at, rows)]]
        offsets += [(j - z - NZ) * rows, jnp.where(later, j - z - 2 * NZ, j - z) * rows]
    copies = [pltpu.make_async_copy(s, kv_ref.at[n], sems.at[n]) for n, s in enumerate(sources)]
    for copy in copies:
        copy.start()
    q, start = heads_below(q_ref, first_ref)
    carry = None
    n = 0
    for size in (1, 4, 4, 4, 4):
        blocks = []
        for i in range(n, n + size):
            copies[i].wait()
            blocks.append((kv_ref[i, :, :HEAD], kv_ref[i, :, HEAD:], offsets[i]))
        carry = merge(q, start, blocks, carry, rows, n == 0)
        n += size
    o = (carry[2] / carry[1]).astype(BF)
    out_ref[:, :HEAD] = o[:rows]
    out_ref[:, HEAD:] = o[rows:]


def project_kernel(attn_ref, ssm_ref, wa_ref, ws_ref, out_ref):
    width = out_ref.shape[2]
    out = mm(attn_ref[...], wa_ref[...]) + mm(ssm_ref[...], ws_ref[...])
    for i in range(NC):
        out_ref[i] = out[:, i * width : (i + 1) * width].astype(BF)


def project(attn, ssm, wa, ws):
    rows, width = attn.shape[0], wa.shape[1] // NX
    return call(
        project_kernel,
        jax.ShapeDtypeStruct((NX * NC, rows, width // NC), BF),
        cost(2 * rows * 768 * wa.shape[1], 2 * 768 * wa.shape[1]),
        WIDE,
        grid=(NX,),
        in_specs=[
            pl.BlockSpec(attn.shape, lambda j: (0, 0)),
            pl.BlockSpec(ssm.shape, lambda j: (0, 0)),
            pl.BlockSpec((wa.shape[0], width), lambda j: (0, j)),
            pl.BlockSpec((ws.shape[0], width), lambda j: (0, j)),
        ],
        out_specs=pl.BlockSpec((NC, rows, width // NC), lambda j: (j, 0, 0)),
    )(attn, ssm, wa, ws)


def halves_kernel(a_ref, b_ref, top_ref, rest_ref):
    half = top_ref.shape[0]
    top_ref[...] = a_ref[:half]
    rest_ref[...] = b_ref[half:]


def total_kernel(right_ref, left_ref, own_ref, attn_ref, ssm_ref):
    split = ssm_ref.shape[1]
    for ref, cols in ((ssm_ref, slice(0, split)), (attn_ref, slice(split, None))):
        ref[...] = right_ref[:, cols].astype(F32) + left_ref[:, cols].astype(F32) + own_ref[:, cols].astype(F32)


def grads_kernel(at_ref, *refs):
    z, c = at_ref[0], at_ref[1]
    mine, other, joined, out_ref = refs[:NY], refs[NY : 2 * NY], refs[2 * NY : -1], refs[-1]
    begin = 0
    if joined[-1].shape[0] == NZ:
        *joined, done_ref = joined
        begin = done_ref.shape[2]
        out_ref[:, :, :begin] = done_ref[...]
    rows = out_ref.shape[1]
    value = jnp.concatenate([r[...] for r in joined], axis=0)
    for half, core in ((mine, c), (other, 1 - c)):
        cot = jnp.concatenate([r[...] for r in half], axis=0)
        t = mm(cot, value, ((0,), (0,))).astype(BF)
        for i in range(NZ // NC):
            slot = lax.rem(core * (NZ // NC) + i - z + NZ, NZ)
            out_ref[slot, :, begin:] = t[i * rows : (i + 1) * rows]


def add(a, b):
    return (a.astype(F32) + b.astype(F32)).astype(BF)


class Ring:
    def __init__(self, terms):
        self.terms = terms
        self.right, self.left = terms[4], terms[NZ - 3]
        self.count = 0

    def step(self):
        k = self.count
        right = shift(self.right, "z", 1)
        if k < 3:
            left = shift(self.left, "z", -1)
            self.left = add(left, self.terms[NZ + k - 2]) if k < 2 else left
        self.right = add(right, self.terms[3 - k]) if k < 3 else right
        self.count = k + 1


def after(*values):
    return lax.optimization_barrier(values)


def body(
    lengths,
    queries,
    keys,
    values,
    ssm_input,
    gate_input,
    b_input,
    c_input,
    log_decay,
    skip,
    norm_gain,
    attn_out_weight,
    ssm_out_weight,
    cotangent,
):
    rows, width = queries.shape[0], cotangent.shape[1]
    x, c, y, z = (lax.axis_index(a) for a in ("x", "c", "y", "z"))
    scalar = lambda v: jnp.full((1,), v, jnp.int32)
    smem = pl.BlockSpec(memory_space=pltpu.SMEM)
    vmem = pl.BlockSpec(memory_space=pltpu.VMEM)
    shape = jax.ShapeDtypeStruct

    kv = jnp.concatenate([keys, values], axis=1)
    far8, far16 = shift(kv, YZ, 8, False), shift(kv, YZ, 16, False)
    anywhere = pl.BlockSpec(memory_space=pl.ANY)
    y_local, packed, cum, first = call(
        ssm_first,
        (
            shape((rows, 512), F32),
            shape((SN, 640), BF),
            shape((rows, 128), F32),
            shape((rows, 1), jnp.int32),
        ),
        cost(2 * rows * rows * 128 * 10, 2**21, 8 * rows * rows),
        WIDE,
        in_specs=[smem] + [anywhere] * 6,
        scratch_shapes=[
            pltpu.SMEM((32,), jnp.int32),
            pltpu.VMEM((rows, 512), BF),
            pltpu.VMEM((rows, SN), BF),
            pltpu.VMEM((rows, SN), BF),
            pltpu.VMEM((8, rows), F32),
            pltpu.VMEM((1, 8), F32),
            pltpu.SemaphoreType.DMA((6,)),
        ],
    )(scalar((y * NZ + z) * rows), lengths, ssm_input, b_input, c_input, log_decay.T, skip[None, :])
    far8, far16, packed, first, queries, cotangent = after(far8, far16, packed, first, queries, cotangent)
    blocks = lax.all_gather(jnp.concatenate([kv, far8, far16], axis=0), "z")

    cots = [cotangent] + [shift(cotangent, "x", k) for k in range(1, NX)]
    slices = lax.all_to_all(packed.reshape(NZ, 16, 640), "z", 0, 0)
    inside, products, row_total = call(
        ssm_scan,
        (shape((NZ, 16, 512), F32), shape((NZ, 512), F32), shape((16, 640), BF)),
    )(slices)
    one, two = shift(row_total, "y", 1, False), shift(row_total, "y", 2, False)
    joined = call(ssm_join, shape((NZ, 16, 512), BF))(inside, products, one, two)
    joined, cots = after(joined, cots)
    piece = shape((rows, width), BF)
    slabs = call(pick_kernel, (piece,) * NY, cost(0, 2**21), in_specs=[smem] + [vmem] * NX)(
        jnp.stack([(x - y - k) % NX for k in range(NY)]).astype(jnp.int32), *cots
    )
    mine = [slabs[0]] + [shift(slabs[k], "y", k) for k in range(1, NY)]
    state_in = lax.all_to_all(joined, "z", 0, 0).reshape(SN, 512)
    ssm_out = call(
        ssm_last, shape((rows, 512), BF), cost(2 * rows * 128 * 512, 2**20, rows * 512)
    )(c_input, state_in, y_local, cum, first, gate_input, norm_gain[None, :])
    ssm_out, mine = after(ssm_out, mine)

    ssm_next, ssm_prev = shift(ssm_out, "y", 1), shift(ssm_out, "y", -1)
    attn_out = call(
        attn_kernel,
        shape((rows, 2 * HEAD), BF),
        cost(17 * 8 * rows * rows * HEAD, 2**22, 34 * rows * rows),
        WIDE,
        in_specs=[smem, anywhere] + [vmem] * 2,
        scratch_shapes=[
            pltpu.VMEM((2 * NZ + 1, rows, 2 * HEAD), BF),
            pltpu.SemaphoreType.DMA((2 * NZ + 1,)),
        ],
    )(scalar(z), blocks, queries, first)
    ssm_next, ssm_prev, attn_out = after(ssm_next, ssm_prev, attn_out)
    all_attn = [attn_out] + [shift(attn_out, "y", k) for k in range(1, NY)]
    other = [shift(m, "c", 1) for m in mine]
    half = shape((rows // 2, 512), BF)
    top, rest = call(halves_kernel, (half, half), cost(0, 2**19))(ssm_next, ssm_prev)
    top, rest = shift(top, "y", 1), shift(rest, "y", -1)
    all_ssm = [ssm_out, ssm_next, top, rest, ssm_prev]
    index = jnp.stack([z, c]).astype(jnp.int32)
    terms = call(
        grads_kernel,
        shape((NZ, 160, 512), BF),
        cost(2 * 1280 * 1024 * 512, 2**23),
        in_specs=[smem] + [vmem] * (2 * NY + len(all_ssm)),
    )(index, *mine, *other, *all_ssm)
    pieces = project(attn_out, ssm_out, attn_out_weight, ssm_out_weight)
    pieces, *all_attn = after(pieces, *all_attn)
    mixed = lax.psum_scatter(pieces, ("x", "c"), scatter_dimension=0, tiled=False)
    terms = call(
        grads_kernel,
        shape((NZ, 160, 768), BF),
        cost(2 * 1280 * 1024 * 256, 2**23),
        in_specs=[smem] + [vmem] * (3 * NY + 1),
    )(index, *mine, *other, *all_attn, terms)
    ring = Ring(terms)
    for _ in range(4):
        ring.step()
    grad_attn, grad_ssm = call(
        total_kernel, (shape((160, 256), F32), shape((160, 512), F32)), cost(0, 2**20)
    )(ring.right, ring.left, terms[0])
    return mixed, grad_attn, grad_ssm


def solution(mesh):
    fine = Mesh(mesh.devices.reshape(NY, NZ, NX, NC), ("y", "z", "x", "c"))
    tp = ("x", "c")
    both = P(YZ, tp)
    placed = (P(),) + (both,) * 8 + (P(tp), P(tp), P(tp, None), P(tp, None), both)
    return jax.shard_map(
        body, mesh=fine, in_specs=placed, out_specs=(both, both, both), check_vma=False
    )
```

```python
import functools

import jax
import jax.numpy as jnp
from jax import lax
from jax.experimental import pallas as pl
from jax.experimental.pallas import tpu as pltpu
from jax.sharding import Mesh
from jax.sharding import PartitionSpec as P

HEAD = 128
GRP = 2
SP = 64
SN = 128
NY = 4
NZ = 8
NX = 4
NC = 2
YZ = ("y", "z")
F32 = jnp.float32
BF = jnp.bfloat16
HI = lax.Precision.HIGHEST
LOW = -1e30
LOG2E = 1.4426950408889634
SPLIT = 2
LIMIT = 16 * 1024 * 1024
WIDE = 54 * 1024 * 1024


def shift(value, axis, steps, cyclic=True):
    n = lax.axis_size(axis)
    pairs = [(i, (i + steps) % n) for i in range(n) if cyclic or 0 <= i + steps < n]
    return lax.ppermute(value, axis, pairs)


def call(kernel, outs, cost=None, limit=LIMIT, **kw):
    return pl.pallas_call(
        kernel,
        out_shape=outs,
        compiler_params=pltpu.CompilerParams(vmem_limit_bytes=limit),
        cost_estimate=cost,
        **kw,
    )


def cost(flops, nbytes, exps=0):
    return pl.CostEstimate(flops=int(flops), bytes_accessed=int(nbytes), transcendentals=int(exps))


def mm(a, b, dims=((1,), (0,)), precision=None):
    return lax.dot_general(a, b, (dims, ((), ())), preferred_element_type=F32, precision=precision)


def spread(pairs, lane):
    return jnp.where(lane < SP, pairs[0], pairs[1])


def ssm_first(
    base_ref, len_hbm, x_hbm, b_hbm, c_hbm, ld_hbm, skip_hbm, y_ref, state_ref, cum_ref, first_ref,
    len_ref, x_ref, b_ref, c_ref, ld_ref, skip_ref, sems,
):
    pairs = [(ld_hbm, ld_ref), (len_hbm, len_ref), (b_hbm, b_ref), (c_hbm, c_ref), (x_hbm, x_ref), (skip_hbm, skip_ref)]
    copies = [pltpu.make_async_copy(src, dst, sems.at[i]) for i, (src, dst) in enumerate(pairs)]
    for copy in copies:
        copy.start()
    for copy in copies:
        copy.wait()
    rows = x_ref.shape[0]
    r1 = lax.broadcasted_iota(jnp.int32, (rows, 1), 0)
    base = base_ref[0]
    begin, first = jnp.int32(0), jnp.zeros((rows, 1), jnp.int32) - base
    for j in range(len_ref.shape[0]):
        first = jnp.where(r1 + base >= begin, begin - base, first)
        begin = begin + len_ref[j]
    first_ref[...] = first
    row = lax.broadcasted_iota(jnp.int32, (rows, rows), 0)
    col = lax.broadcasted_iota(jnp.int32, (rows, rows), 1)
    lower = jnp.where(col <= row, 1.0, 0.0).astype(F32)
    heads = ld_ref.shape[0]
    l = lax.broadcasted_iota(jnp.int32, (128, heads), 0)
    h = lax.broadcasted_iota(jnp.int32, (128, heads), 1)
    decays = mm(jnp.where(h == l, 1.0, 0.0).astype(F32), ld_ref[...], precision=HI)
    cum = mm(lower, decays, ((1,), (1,)), precision=HI)
    cum_ref[...] = cum
    cum_t = cum.T
    mask = (col <= row) & (col >= first)
    inner = mm(c_ref[...], b_ref[...], ((1,), (1,)))
    last = cum[rows - 1 : rows, :]
    last_first = first[rows - 1 : rows, :]
    tail = jnp.where(r1 >= last_first, jnp.exp(last - cum), 0.0)
    lane = lax.broadcasted_iota(jnp.int32, (rows, 2 * SP), 1)
    b_t = b_ref[...].astype(F32).T.astype(BF)
    skip = mm(skip_ref[...], heads_matrix(heads), precision=HI)
    for p in range(4):
        x = x_ref[:, p * 128 : (p + 1) * 128]
        y = []
        for h in (2 * p, 2 * p + 1):
            diff = jnp.where(mask, cum[:, h : h + 1] - cum_t[h : h + 1, :], LOW)
            mixing = (jnp.exp(diff) * inner).astype(BF)
            y.append(mm(mixing, x))
        xf = x.astype(F32)
        y_ref[:, p * 128 : (p + 1) * 128] = spread(y, lane) + skip[:, p * 128 : (p + 1) * 128] * xf
        scaled = spread([tail[:, 2 * p : 2 * p + 1], tail[:, 2 * p + 1 : 2 * p + 2]], lane) * xf
        state_ref[:, p * 128 : (p + 1) * 128] = mm(b_t, scaled.astype(BF)).astype(BF)
    total = jnp.where(last_first < 0, jnp.exp(last), 0.0)
    high = total.astype(BF).astype(F32)
    r2 = lax.broadcasted_iota(jnp.int32, (SN, 128), 0)
    state_ref[:, 512:] = jnp.where(r2 % 16 < 8, high, total - high).astype(BF)


def heads_matrix(n=128):
    h = lax.broadcasted_iota(jnp.int32, (n, 512), 0)
    l = lax.broadcasted_iota(jnp.int32, (n, 512), 1)
    return jnp.where((l >= h * SP) & (l < (h + 1) * SP), 1.0, 0.0).astype(F32)


def unpack_total(block):
    side = block[:, 512:].astype(F32)
    return side[0:1, :] + side[8:9, :]


def ssm_scan(g_ref, e_ref, p_ref, r_ref):
    totals = jnp.concatenate([unpack_total(g_ref[i]) for i in range(NZ)], axis=0)
    wide = mm(totals, heads_matrix(), precision=HI)
    acc = jnp.zeros((16, 512), F32)
    prod = jnp.ones((1, 512), F32)
    small = jnp.ones((1, 128), F32)
    for i in range(NZ):
        e_ref[i] = acc
        p_ref[i : i + 1, :] = prod
        t = wide[i : i + 1, :]
        acc = t * acc + g_ref[i][:, :512].astype(F32)
        prod = prod * t
        small = small * totals[i : i + 1, :]
    r_ref[:, :512] = acc.astype(BF)
    high = small.astype(BF).astype(F32)
    r2 = lax.broadcasted_iota(jnp.int32, (16, 128), 0)
    r_ref[:, 512:] = jnp.where(r2 < 8, high, small - high).astype(BF)


def ssm_join(e_ref, p_ref, one_ref, two_ref, out_ref):
    one, two = one_ref[...], two_ref[...]
    total = jnp.broadcast_to(unpack_total(one), (8, 128))
    wide = mm(total, heads_matrix(), precision=HI)[0:1, :]
    carry = one[:, :512].astype(F32) + wide * two[:, :512].astype(F32)
    for i in range(NZ):
        out_ref[i] = (e_ref[i] + p_ref[i : i + 1, :] * carry).astype(BF)


def ssm_last(c_ref, state_ref, y_ref, cum_ref, first_ref, gate_ref, gain_ref, out_ref):
    rows = c_ref.shape[0]
    reach = jnp.where(first_ref[...] < 0, jnp.exp(cum_ref[...]), 0.0)
    lane = lax.broadcasted_iota(jnp.int32, (rows, 2 * SP), 1)
    gated = []
    squares = jnp.zeros((rows, 1), F32)
    for p in range(4):
        cols = slice(p * 128, (p + 1) * 128)
        carried = mm(c_ref[...], state_ref[:, cols])
        carried = carried * spread([reach[:, 2 * p : 2 * p + 1], reach[:, 2 * p + 1 : 2 * p + 2]], lane)
        gate = gate_ref[:, cols].astype(F32)
        u = (y_ref[:, cols] + carried) * (gate / (1.0 + jnp.exp(-gate)))
        squares = squares + jnp.sum(u * u, axis=1, keepdims=True)
        gated.append(u)
    scale = lax.rsqrt(squares / 512.0 + 1e-05)
    for p in range(4):
        cols = slice(p * 128, (p + 1) * 128)
        out_ref[:, cols] = (gated[p] * scale * gain_ref[:, cols]).astype(BF)


def pick_kernel(at_ref, *refs):
    for k in range(NY):
        for j in range(NX):

            @pl.when(at_ref[k] == j)
            def _():
                refs[NX + k][...] = refs[j][...]


def merge(q, start, blocks, carry, rows, causal_first=False):
    col = lax.broadcasted_iota(jnp.int32, (2 * rows, rows), 1)
    scores = []
    for i, (key, _, offset) in enumerate(blocks):
        s = mm(q, key, ((1,), (1,))) * (HEAD**-0.5 * LOG2E)
        allowed = col >= start - offset
        if causal_first and i == 0:
            row = lax.broadcasted_iota(jnp.int32, (rows, rows), 0)
            allowed = allowed & (col <= jnp.concatenate([row, row], axis=0))
        scores.append(jnp.where(allowed, s, LOW))
    top = functools.reduce(jnp.maximum, scores)
    m = jnp.max(top, axis=1, keepdims=True)
    if carry is not None:
        m = jnp.maximum(m, carry[0])
    p = [jnp.exp2(s - m) for s in scores]
    l = jnp.sum(functools.reduce(jnp.add, p), axis=1, keepdims=True)
    a = functools.reduce(jnp.add, [mm(w.astype(BF), v) for w, (_, v, _) in zip(p, blocks)])
    if carry is not None:
        factor = jnp.exp2(carry[0] - m)
        l, a = l + carry[1] * factor, a + carry[2] * factor
    return m, l, a


def heads_below(q_ref, first_ref):
    q = jnp.concatenate([q_ref[:, :HEAD], q_ref[:, HEAD:]], axis=0)
    start = first_ref[...]
    return q, jnp.concatenate([start, start], axis=0)


def attn_kernel(z_ref, kv_hbm, q_ref, first_ref, out_ref, kv_ref, sems):
    rows = q_ref.shape[0]
    z = z_ref[0]
    sources = [kv_hbm.at[z, pl.ds(0, rows)]]
    offsets = [jnp.int32(0)]
    for j in range(NZ):
        later = j >= z
        at = pl.multiple_of(jnp.where(later, 2 * rows, 0), rows)
        sources += [kv_hbm.at[j, pl.ds(rows, rows)], kv_hbm.at[j, pl.ds(at, rows)]]
        offsets += [(j - z - NZ) * rows, jnp.where(later, j - z - 2 * NZ, j - z) * rows]
    copies = [pltpu.make_async_copy(s, kv_ref.at[n], sems.at[n]) for n, s in enumerate(sources)]
    for copy in copies:
        copy.start()
    q, start = heads_below(q_ref, first_ref)
    carry = None
    n = 0
    for size in (1, 4, 4, 4, 4):
        blocks = []
        for i in range(n, n + size):
            copies[i].wait()
            blocks.append((kv_ref[i, :, :HEAD], kv_ref[i, :, HEAD:], offsets[i]))
        carry = merge(q, start, blocks, carry, rows, n == 0)
        n += size
    o = (carry[2] / carry[1]).astype(BF)
    out_ref[:, :HEAD] = o[:rows]
    out_ref[:, HEAD:] = o[rows:]


def project_kernel(attn_ref, ssm_ref, wa_ref, ws_ref, out_ref):
    width = out_ref.shape[2]
    out = mm(attn_ref[...], wa_ref[...]) + mm(ssm_ref[...], ws_ref[...])
    for i in range(NC):
        out_ref[i] = out[:, i * width : (i + 1) * width].astype(BF)


def project(attn, ssm, wa, ws):
    rows, width = attn.shape[0], wa.shape[1] // NX
    return call(
        project_kernel,
        jax.ShapeDtypeStruct((NX * NC, rows, width // NC), BF),
        cost(2 * rows * 768 * wa.shape[1], 2 * 768 * wa.shape[1]),
        WIDE,
        grid=(NX,),
        in_specs=[
            pl.BlockSpec(attn.shape, lambda j: (0, 0)),
            pl.BlockSpec(ssm.shape, lambda j: (0, 0)),
            pl.BlockSpec((wa.shape[0], width), lambda j: (0, j)),
            pl.BlockSpec((ws.shape[0], width), lambda j: (0, j)),
        ],
        out_specs=pl.BlockSpec((NC, rows, width // NC), lambda j: (j, 0, 0)),
    )(attn, ssm, wa, ws)


def stack_kernel(*refs):
    for k in range(NY):
        refs[NY][k] = refs[k][...]


def halves_kernel(a_ref, b_ref, top_ref, rest_ref):
    half = top_ref.shape[0]
    top_ref[...] = a_ref[:half]
    rest_ref[...] = b_ref[half:]


def total_kernel(right_ref, left_ref, own_ref, attn_ref, ssm_ref):
    split = ssm_ref.shape[1]
    for ref, cols in ((ssm_ref, slice(0, split)), (attn_ref, slice(split, None))):
        ref[...] = right_ref[:, cols].astype(F32) + left_ref[:, cols].astype(F32) + own_ref[:, cols].astype(F32)


def grads_kernel(at_ref, *refs):
    z, c = at_ref[0], at_ref[1]
    mine, other, joined, out_ref = refs[0], refs[1], refs[2:-1], refs[-1]
    begin = 0
    if joined[-1].shape[0] == NZ:
        *joined, done_ref = joined
        begin = done_ref.shape[2]
        out_ref[:, :, :begin] = done_ref[...]
    rows = out_ref.shape[1]
    value = jnp.concatenate([r[...] for r in joined], axis=0)
    for half, core in ((mine, c), (other, 1 - c)):
        cot = half[...].reshape(half.shape[0] * half.shape[1], half.shape[2])
        t = mm(cot, value, ((0,), (0,))).astype(BF)
        for i in range(NZ // NC):
            slot = lax.rem(core * (NZ // NC) + i - z + NZ, NZ)
            out_ref[slot, :, begin:] = t[i * rows : (i + 1) * rows]


def add(a, b):
    return (a.astype(F32) + b.astype(F32)).astype(BF)


class Ring:
    def __init__(self, terms):
        self.terms = terms
        self.right, self.left = terms[4], terms[NZ - 3]
        self.count = 0

    def step(self):
        k = self.count
        right = shift(self.right, "z", 1)
        if k < 3:
            left = shift(self.left, "z", -1)
            self.left = add(left, self.terms[NZ + k - 2]) if k < 2 else left
        self.right = add(right, self.terms[3 - k]) if k < 3 else right
        self.count = k + 1


def after(*values):
    return lax.optimization_barrier(values)


def body(
    lengths,
    queries,
    keys,
    values,
    ssm_input,
    gate_input,
    b_input,
    c_input,
    log_decay,
    skip,
    norm_gain,
    attn_out_weight,
    ssm_out_weight,
    cotangent,
):
    rows, width = queries.shape[0], cotangent.shape[1]
    x, c, y, z = (lax.axis_index(a) for a in ("x", "c", "y", "z"))
    scalar = lambda v: jnp.full((1,), v, jnp.int32)
    smem = pl.BlockSpec(memory_space=pltpu.SMEM)
    vmem = pl.BlockSpec(memory_space=pltpu.VMEM)
    shape = jax.ShapeDtypeStruct

    kv = jnp.concatenate([keys, values], axis=1)
    far8, far16 = shift(kv, YZ, 8, False), shift(kv, YZ, 16, False)
    anywhere = pl.BlockSpec(memory_space=pl.ANY)
    y_local, packed, cum, first = call(
        ssm_first,
        (
            shape((rows, 512), F32),
            shape((SN, 640), BF),
            shape((rows, 128), F32),
            shape((rows, 1), jnp.int32),
        ),
        cost(2 * rows * rows * 128 * 10, 2**21, 8 * rows * rows),
        WIDE,
        in_specs=[smem] + [anywhere] * 6,
        scratch_shapes=[
            pltpu.SMEM((32,), jnp.int32),
            pltpu.VMEM((rows, 512), BF),
            pltpu.VMEM((rows, SN), BF),
            pltpu.VMEM((rows, SN), BF),
            pltpu.VMEM((8, rows), F32),
            pltpu.VMEM((1, 8), F32),
            pltpu.SemaphoreType.DMA((6,)),
        ],
    )(scalar((y * NZ + z) * rows), lengths, ssm_input, b_input, c_input, log_decay.T, skip[None, :])
    far8, far16, packed, first, queries, cotangent = after(far8, far16, packed, first, queries, cotangent)
    blocks = lax.all_gather(jnp.concatenate([kv, far8, far16], axis=0), "z")

    cots = [cotangent] + [shift(cotangent, "x", k) for k in range(1, NX)]
    slices = lax.all_to_all(packed.reshape(NZ, 16, 640), "z", 0, 0)
    inside, products, row_total = call(
        ssm_scan,
        (shape((NZ, 16, 512), F32), shape((NZ, 512), F32), shape((16, 640), BF)),
    )(slices)
    one, two = shift(row_total, "y", 1, False), shift(row_total, "y", 2, False)
    joined = call(ssm_join, shape((NZ, 16, 512), BF))(inside, products, one, two)
    piece = shape((rows, width), BF)
    slabs = call(pick_kernel, (piece,) * NY, cost(0, 2**21), in_specs=[smem] + [vmem] * NX)(
        jnp.stack([(x - y - k) % NX for k in range(NY)]).astype(jnp.int32), *cots
    )
    mine = [slabs[0]] + [shift(slabs[k], "y", k) for k in range(1, NY)]
    state_in = lax.all_to_all(joined, "z", 0, 0).reshape(SN, 512)
    ssm_out = call(
        ssm_last, shape((rows, 512), BF), cost(2 * rows * 128 * 512, 2**20, rows * 512)
    )(c_input, state_in, y_local, cum, first, gate_input, norm_gain[None, :])

    ssm_next, ssm_prev = shift(ssm_out, "y", 1), shift(ssm_out, "y", -1)
    attn_out = call(
        attn_kernel,
        shape((rows, 2 * HEAD), BF),
        cost(17 * 8 * rows * rows * HEAD, 2**22, 34 * rows * rows),
        WIDE,
        in_specs=[smem, anywhere] + [vmem] * 2,
        scratch_shapes=[
            pltpu.VMEM((2 * NZ + 1, rows, 2 * HEAD), BF),
            pltpu.SemaphoreType.DMA((2 * NZ + 1,)),
        ],
    )(scalar(z), blocks, queries, first)
    ssm_next, ssm_prev, attn_out, mine = after(ssm_next, ssm_prev, attn_out, mine)
    all_attn = [attn_out] + [shift(attn_out, "y", k) for k in range(1, NY)]
    mine = call(
        stack_kernel, shape((NY, rows, width), BF), cost(0, 2**21), in_specs=[vmem] * NY
    )(*mine)
    other = shift(mine, "c", 1)
    half = shape((rows // 2, 512), BF)
    top, rest = call(halves_kernel, (half, half), cost(0, 2**19))(ssm_next, ssm_prev)
    top, rest = shift(top, "y", 1), shift(rest, "y", -1)
    ready, top, rest, other = after(attn_out, top, rest, other)
    all_ssm = [ssm_out, ssm_next, top, rest, ssm_prev]
    index = jnp.stack([z, c]).astype(jnp.int32)
    terms = call(
        grads_kernel,
        shape((NZ, 160, 512), BF),
        cost(2 * 1280 * 1024 * 512, 2**23),
        in_specs=[smem] + [vmem] * (2 + len(all_ssm)),
    )(index, mine, other, *all_ssm)
    pieces = project(ready, ssm_out, attn_out_weight, ssm_out_weight)
    pieces, *all_attn = after(pieces, *all_attn)
    mixed = lax.psum_scatter(pieces, ("x", "c"), scatter_dimension=0, tiled=False)
    terms = call(
        grads_kernel,
        shape((NZ, 160, 768), BF),
        cost(2 * 1280 * 1024 * 256, 2**23),
        in_specs=[smem] + [vmem] * (2 + NY + 1),
    )(index, mine, other, *all_attn, terms)
    ring = Ring(terms)
    for _ in range(4):
        ring.step()
    grad_attn, grad_ssm = call(
        total_kernel, (shape((160, 256), F32), shape((160, 512), F32)), cost(0, 2**20)
    )(ring.right, ring.left, terms[0])
    return mixed, grad_attn, grad_ssm


def solution(mesh):
    fine = Mesh(mesh.devices.reshape(NY, NZ, NX, NC), ("y", "z", "x", "c"))
    tp = ("x", "c")
    both = P(YZ, tp)
    placed = (P(),) + (both,) * 8 + (P(tp), P(tp), P(tp, None), P(tp, None), both)
    return jax.shard_map(
        body, mesh=fine, in_specs=placed, out_specs=(both, both, both), check_vma=False
    )
```

```python
import functools

import jax
import jax.numpy as jnp
from jax import lax
from jax.experimental import pallas as pl
from jax.experimental.pallas import tpu as pltpu
from jax.sharding import Mesh
from jax.sharding import PartitionSpec as P

HEAD = 128
GRP = 2
SP = 64
SN = 128
NY = 4
NZ = 8
NX = 4
NC = 2
YZ = ("y", "z")
F32 = jnp.float32
BF = jnp.bfloat16
HI = lax.Precision.HIGHEST
LOW = -1e30
LOG2E = 1.4426950408889634
SPLIT = 2
LIMIT = 16 * 1024 * 1024
WIDE = 54 * 1024 * 1024


def shift(value, axis, steps, cyclic=True):
    n = lax.axis_size(axis)
    pairs = [(i, (i + steps) % n) for i in range(n) if cyclic or 0 <= i + steps < n]
    return lax.ppermute(value, axis, pairs)


def call(kernel, outs, cost=None, limit=LIMIT, **kw):
    return pl.pallas_call(
        kernel,
        out_shape=outs,
        compiler_params=pltpu.CompilerParams(vmem_limit_bytes=limit),
        cost_estimate=cost,
        **kw,
    )


def cost(flops, nbytes, exps=0):
    return pl.CostEstimate(flops=int(flops), bytes_accessed=int(nbytes), transcendentals=int(exps))


def mm(a, b, dims=((1,), (0,)), precision=None):
    return lax.dot_general(a, b, (dims, ((), ())), preferred_element_type=F32, precision=precision)


def spread(pairs, lane):
    return jnp.where(lane < SP, pairs[0], pairs[1])


def ssm_first(
    base_ref, len_hbm, x_hbm, b_hbm, c_hbm, ld_hbm, skip_hbm, y_ref, state_ref, cum_ref, first_ref,
    len_ref, x_ref, b_ref, c_ref, ld_ref, skip_ref, sems,
):
    pairs = [(ld_hbm, ld_ref), (len_hbm, len_ref), (b_hbm, b_ref), (c_hbm, c_ref), (x_hbm, x_ref), (skip_hbm, skip_ref)]
    copies = [pltpu.make_async_copy(src, dst, sems.at[i]) for i, (src, dst) in enumerate(pairs)]
    for copy in copies:
        copy.start()
    for copy in copies:
        copy.wait()
    rows = x_ref.shape[0]
    r1 = lax.broadcasted_iota(jnp.int32, (rows, 1), 0)
    base = base_ref[0]
    begin, first = jnp.int32(0), jnp.zeros((rows, 1), jnp.int32) - base
    for j in range(len_ref.shape[0]):
        first = jnp.where(r1 + base >= begin, begin - base, first)
        begin = begin + len_ref[j]
    first_ref[...] = first
    row = lax.broadcasted_iota(jnp.int32, (rows, rows), 0)
    col = lax.broadcasted_iota(jnp.int32, (rows, rows), 1)
    lower = jnp.where(col <= row, 1.0, 0.0).astype(F32)
    heads = ld_ref.shape[0]
    l = lax.broadcasted_iota(jnp.int32, (128, heads), 0)
    h = lax.broadcasted_iota(jnp.int32, (128, heads), 1)
    decays = mm(jnp.where(h == l, 1.0, 0.0).astype(F32), ld_ref[...], precision=HI)
    cum = mm(lower, decays, ((1,), (1,)), precision=HI)
    cum_ref[...] = cum
    cum_t = cum.T
    mask = (col <= row) & (col >= first)
    inner = mm(c_ref[...], b_ref[...], ((1,), (1,)))
    last = cum[rows - 1 : rows, :]
    last_first = first[rows - 1 : rows, :]
    tail = jnp.where(r1 >= last_first, jnp.exp(last - cum), 0.0)
    lane = lax.broadcasted_iota(jnp.int32, (rows, 2 * SP), 1)
    b_t = b_ref[...].astype(F32).T.astype(BF)
    skip = mm(skip_ref[...], heads_matrix(heads), precision=HI)
    for p in range(4):
        x = x_ref[:, p * 128 : (p + 1) * 128]
        y = []
        for h in (2 * p, 2 * p + 1):
            diff = jnp.where(mask, cum[:, h : h + 1] - cum_t[h : h + 1, :], LOW)
            mixing = (jnp.exp(diff) * inner).astype(BF)
            y.append(mm(mixing, x))
        xf = x.astype(F32)
        y_ref[:, p * 128 : (p + 1) * 128] = spread(y, lane) + skip[:, p * 128 : (p + 1) * 128] * xf
        scaled = spread([tail[:, 2 * p : 2 * p + 1], tail[:, 2 * p + 1 : 2 * p + 2]], lane) * xf
        state_ref[:, p * 128 : (p + 1) * 128] = mm(b_t, scaled.astype(BF)).astype(BF)
    total = jnp.where(last_first < 0, jnp.exp(last), 0.0)
    high = total.astype(BF).astype(F32)
    r2 = lax.broadcasted_iota(jnp.int32, (SN, 128), 0)
    state_ref[:, 512:] = jnp.where(r2 % 16 < 8, high, total - high).astype(BF)


def heads_matrix(n=128):
    h = lax.broadcasted_iota(jnp.int32, (n, 512), 0)
    l = lax.broadcasted_iota(jnp.int32, (n, 512), 1)
    return jnp.where((l >= h * SP) & (l < (h + 1) * SP), 1.0, 0.0).astype(F32)


def unpack_total(block):
    side = block[:, 512:].astype(F32)
    return side[0:1, :] + side[8:9, :]


def ssm_scan(g_ref, e_ref, p_ref, r_ref):
    totals = jnp.concatenate([unpack_total(g_ref[i]) for i in range(NZ)], axis=0)
    wide = mm(totals, heads_matrix(), precision=HI)
    acc = jnp.zeros((16, 512), F32)
    prod = jnp.ones((1, 512), F32)
    small = jnp.ones((1, 128), F32)
    for i in range(NZ):
        e_ref[i] = acc
        p_ref[i : i + 1, :] = prod
        t = wide[i : i + 1, :]
        acc = t * acc + g_ref[i][:, :512].astype(F32)
        prod = prod * t
        small = small * totals[i : i + 1, :]
    r_ref[:, :512] = acc.astype(BF)
    high = small.astype(BF).astype(F32)
    r2 = lax.broadcasted_iota(jnp.int32, (16, 128), 0)
    r_ref[:, 512:] = jnp.where(r2 < 8, high, small - high).astype(BF)


def ssm_join(e_ref, p_ref, one_ref, two_ref, out_ref):
    one, two = one_ref[...], two_ref[...]
    total = jnp.broadcast_to(unpack_total(one), (8, 128))
    wide = mm(total, heads_matrix(), precision=HI)[0:1, :]
    carry = one[:, :512].astype(F32) + wide * two[:, :512].astype(F32)
    for i in range(NZ):
        out_ref[i] = (e_ref[i] + p_ref[i : i + 1, :] * carry).astype(BF)


def ssm_last(c_ref, state_ref, y_ref, cum_ref, first_ref, gate_ref, gain_ref, out_ref):
    rows = c_ref.shape[0]
    reach = jnp.where(first_ref[...] < 0, jnp.exp(cum_ref[...]), 0.0)
    lane = lax.broadcasted_iota(jnp.int32, (rows, 2 * SP), 1)
    gated = []
    squares = jnp.zeros((rows, 1), F32)
    for p in range(4):
        cols = slice(p * 128, (p + 1) * 128)
        carried = mm(c_ref[...], state_ref[:, cols])
        carried = carried * spread([reach[:, 2 * p : 2 * p + 1], reach[:, 2 * p + 1 : 2 * p + 2]], lane)
        gate = gate_ref[:, cols].astype(F32)
        u = (y_ref[:, cols] + carried) * (gate / (1.0 + jnp.exp(-gate)))
        squares = squares + jnp.sum(u * u, axis=1, keepdims=True)
        gated.append(u)
    scale = lax.rsqrt(squares / 512.0 + 1e-05)
    for p in range(4):
        cols = slice(p * 128, (p + 1) * 128)
        out_ref[:, cols] = (gated[p] * scale * gain_ref[:, cols]).astype(BF)


def pick_kernel(at_ref, *refs):
    for k in range(NY):
        for j in range(NX):

            @pl.when(at_ref[k] == j)
            def _():
                refs[NX + k][...] = refs[j][...]


def merge(q, start, blocks, carry, rows, causal_first=False):
    col = lax.broadcasted_iota(jnp.int32, (2 * rows, rows), 1)
    scores = []
    for i, (key, _, offset) in enumerate(blocks):
        s = mm(q, key, ((1,), (1,))) * (HEAD**-0.5 * LOG2E)
        allowed = col >= start - offset
        if causal_first and i == 0:
            row = lax.broadcasted_iota(jnp.int32, (rows, rows), 0)
            allowed = allowed & (col <= jnp.concatenate([row, row], axis=0))
        scores.append(jnp.where(allowed, s, LOW))
    top = functools.reduce(jnp.maximum, scores)
    m = jnp.max(top, axis=1, keepdims=True)
    if carry is not None:
        m = jnp.maximum(m, carry[0])
    p = [jnp.exp2(s - m) for s in scores]
    l = jnp.sum(functools.reduce(jnp.add, p), axis=1, keepdims=True)
    a = functools.reduce(jnp.add, [mm(w.astype(BF), v) for w, (_, v, _) in zip(p, blocks)])
    if carry is not None:
        factor = jnp.exp2(carry[0] - m)
        l, a = l + carry[1] * factor, a + carry[2] * factor
    return m, l, a


def heads_below(q_ref, first_ref):
    q = jnp.concatenate([q_ref[:, :HEAD], q_ref[:, HEAD:]], axis=0)
    start = first_ref[...]
    return q, jnp.concatenate([start, start], axis=0)


def attn_kernel(z_ref, kv_hbm, q_ref, first_ref, out_ref, kv_ref, sems):
    rows = q_ref.shape[0]
    z = z_ref[0]
    sources = [kv_hbm.at[z, pl.ds(0, rows)]]
    offsets = [jnp.int32(0)]
    for j in range(NZ):
        later = j >= z
        at = pl.multiple_of(jnp.where(later, 2 * rows, 0), rows)
        sources += [kv_hbm.at[j, pl.ds(rows, rows)], kv_hbm.at[j, pl.ds(at, rows)]]
        offsets += [(j - z - NZ) * rows, jnp.where(later, j - z - 2 * NZ, j - z) * rows]
    copies = [pltpu.make_async_copy(s, kv_ref.at[n], sems.at[n]) for n, s in enumerate(sources)]
    for copy in copies:
        copy.start()
    q, start = heads_below(q_ref, first_ref)
    carry = None
    n = 0
    for size in (1, 4, 4, 4, 4):
        blocks = []
        for i in range(n, n + size):
            copies[i].wait()
            blocks.append((kv_ref[i, :, :HEAD], kv_ref[i, :, HEAD:], offsets[i]))
        carry = merge(q, start, blocks, carry, rows, n == 0)
        n += size
    o = (carry[2] / carry[1]).astype(BF)
    out_ref[:, :HEAD] = o[:rows]
    out_ref[:, HEAD:] = o[rows:]


def project_kernel(attn_ref, ssm_ref, wa_ref, ws_ref, out_ref):
    width = out_ref.shape[2]
    out = mm(attn_ref[...], wa_ref[...]) + mm(ssm_ref[...], ws_ref[...])
    for i in range(NC):
        out_ref[i] = out[:, i * width : (i + 1) * width].astype(BF)


def project(attn, ssm, wa, ws):
    rows, width = attn.shape[0], wa.shape[1] // NX
    return call(
        project_kernel,
        jax.ShapeDtypeStruct((NX * NC, rows, width // NC), BF),
        cost(2 * rows * 768 * wa.shape[1], 2 * 768 * wa.shape[1]),
        49 * 1024 * 1024,
        grid=(NX,),
        in_specs=[
            pl.BlockSpec(attn.shape, lambda j: (0, 0)),
            pl.BlockSpec(ssm.shape, lambda j: (0, 0)),
            pl.BlockSpec((wa.shape[0], width), lambda j: (0, j)),
            pl.BlockSpec((ws.shape[0], width), lambda j: (0, j)),
        ],
        out_specs=pl.BlockSpec((NC, rows, width // NC), lambda j: (j, 0, 0)),
    )(attn, ssm, wa, ws)


def stack_kernel(*refs):
    for k in range(NY):
        refs[NY][k] = refs[k][...]


def halves_kernel(a_ref, b_ref, top_ref, rest_ref):
    half = top_ref.shape[0]
    top_ref[...] = a_ref[:half]
    rest_ref[...] = b_ref[half:]


def total_kernel(right_ref, left_ref, own_ref, attn_ref, ssm_ref):
    split = ssm_ref.shape[1]
    for ref, cols in ((ssm_ref, slice(0, split)), (attn_ref, slice(split, None))):
        ref[...] = right_ref[:, cols].astype(F32) + left_ref[:, cols].astype(F32) + own_ref[:, cols].astype(F32)


def grads_kernel(at_ref, *refs):
    z, c = at_ref[0], at_ref[1]
    mine, other, joined, out_ref = refs[0], refs[1], refs[2:-1], refs[-1]
    begin = 0
    if joined[-1].shape[0] == NZ:
        *joined, done_ref = joined
        begin = done_ref.shape[2]
        out_ref[:, :, :begin] = done_ref[...]
    rows = out_ref.shape[1]
    value = jnp.concatenate([r[...] for r in joined], axis=0)
    for half, core in ((mine, c), (other, 1 - c)):
        cot = half[...].reshape(half.shape[0] * half.shape[1], half.shape[2])
        t = mm(cot, value, ((0,), (0,))).astype(BF)
        for i in range(NZ // NC):
            slot = lax.rem(core * (NZ // NC) + i - z + NZ, NZ)
            out_ref[slot, :, begin:] = t[i * rows : (i + 1) * rows]


def add(a, b):
    return (a.astype(F32) + b.astype(F32)).astype(BF)


class Ring:
    def __init__(self, terms):
        self.terms = terms
        self.right, self.left = terms[4], terms[NZ - 3]
        self.count = 0

    def step(self):
        k = self.count
        right = shift(self.right, "z", 1)
        if k < 3:
            left = shift(self.left, "z", -1)
            self.left = add(left, self.terms[NZ + k - 2]) if k < 2 else left
        self.right = add(right, self.terms[3 - k]) if k < 3 else right
        self.count = k + 1


def after(*values):
    return lax.optimization_barrier(values)


def body(
    lengths,
    queries,
    keys,
    values,
    ssm_input,
    gate_input,
    b_input,
    c_input,
    log_decay,
    skip,
    norm_gain,
    attn_out_weight,
    ssm_out_weight,
    cotangent,
):
    rows, width = queries.shape[0], cotangent.shape[1]
    x, c, y, z = (lax.axis_index(a) for a in ("x", "c", "y", "z"))
    scalar = lambda v: jnp.full((1,), v, jnp.int32)
    smem = pl.BlockSpec(memory_space=pltpu.SMEM)
    vmem = pl.BlockSpec(memory_space=pltpu.VMEM)
    shape = jax.ShapeDtypeStruct

    kv = jnp.concatenate([keys, values], axis=1)
    far8, far16 = shift(kv, YZ, 8, False), shift(kv, YZ, 16, False)
    anywhere = pl.BlockSpec(memory_space=pl.ANY)
    y_local, packed, cum, first = call(
        ssm_first,
        (
            shape((rows, 512), F32),
            shape((SN, 640), BF),
            shape((rows, 128), F32),
            shape((rows, 1), jnp.int32),
        ),
        cost(2 * rows * rows * 128 * 10, 2**21, 8 * rows * rows),
        WIDE,
        in_specs=[smem] + [anywhere] * 6,
        scratch_shapes=[
            pltpu.SMEM((32,), jnp.int32),
            pltpu.VMEM((rows, 512), BF),
            pltpu.VMEM((rows, SN), BF),
            pltpu.VMEM((rows, SN), BF),
            pltpu.VMEM((8, rows), F32),
            pltpu.VMEM((1, 8), F32),
            pltpu.SemaphoreType.DMA((6,)),
        ],
    )(scalar((y * NZ + z) * rows), lengths, ssm_input, b_input, c_input, log_decay.T, skip[None, :])
    far8, far16, packed, first, queries, cotangent = after(far8, far16, packed, first, queries, cotangent)
    blocks = lax.all_gather(jnp.concatenate([kv, far8, far16], axis=0), "z")

    cots = [cotangent] + [shift(cotangent, "x", k) for k in range(1, NX)]
    slices = lax.all_to_all(packed.reshape(NZ, 16, 640), "z", 0, 0)
    inside, products, row_total = call(
        ssm_scan,
        (shape((NZ, 16, 512), F32), shape((NZ, 512), F32), shape((16, 640), BF)),
    )(slices)
    one, two = shift(row_total, "y", 1, False), shift(row_total, "y", 2, False)
    joined = call(ssm_join, shape((NZ, 16, 512), BF))(inside, products, one, two)
    piece = shape((rows, width), BF)
    slabs = call(pick_kernel, (piece,) * NY, cost(0, 2**21), in_specs=[smem] + [vmem] * NX)(
        jnp.stack([(x - y - k) % NX for k in range(NY)]).astype(jnp.int32), *cots
    )
    mine = [slabs[0]] + [shift(slabs[k], "y", k) for k in range(1, NY)]
    state_in = lax.all_to_all(joined, "z", 0, 0).reshape(SN, 512)
    ssm_out = call(
        ssm_last, shape((rows, 512), BF), cost(2 * rows * 128 * 512, 2**20, rows * 512)
    )(c_input, state_in, y_local, cum, first, gate_input, norm_gain[None, :])

    ssm_next, ssm_prev = shift(ssm_out, "y", 1), shift(ssm_out, "y", -1)
    attn_out = call(
        attn_kernel,
        shape((rows, 2 * HEAD), BF),
        cost(17 * 8 * rows * rows * HEAD, 2**22, 34 * rows * rows),
        WIDE,
        in_specs=[smem, anywhere] + [vmem] * 2,
        scratch_shapes=[
            pltpu.VMEM((2 * NZ + 1, rows, 2 * HEAD), BF),
            pltpu.SemaphoreType.DMA((2 * NZ + 1,)),
        ],
    )(scalar(z), blocks, queries, first)
    ssm_next, ssm_prev, attn_out, mine = after(ssm_next, ssm_prev, attn_out, mine)
    all_attn = [attn_out] + [shift(attn_out, "y", k) for k in range(1, NY)]
    mine = call(
        stack_kernel, shape((NY, rows, width), BF), cost(0, 2**21), in_specs=[vmem] * NY
    )(*mine)
    other = shift(mine, "c", 1)
    half = shape((rows // 2, 512), BF)
    top, rest = call(halves_kernel, (half, half), cost(0, 2**19))(ssm_next, ssm_prev)
    top, rest = shift(top, "y", 1), shift(rest, "y", -1)
    ready, top, rest, other = after(attn_out, top, rest, other)
    all_ssm = [ssm_out, ssm_next, top, rest, ssm_prev]
    index = jnp.stack([z, c]).astype(jnp.int32)
    terms = call(
        grads_kernel,
        shape((NZ, 160, 512), BF),
        cost(2 * 1280 * 1024 * 512, 2**23),
        in_specs=[smem] + [vmem] * (2 + len(all_ssm)),
    )(index, mine, other, *all_ssm)
    pieces = project(ready, ssm_out, attn_out_weight, ssm_out_weight)
    pieces, *all_attn = after(pieces, *all_attn)
    mixed = lax.psum_scatter(pieces, ("x", "c"), scatter_dimension=0, tiled=False)
    terms = call(
        grads_kernel,
        shape((NZ, 160, 768), BF),
        cost(2 * 1280 * 1024 * 256, 2**23),
        in_specs=[smem] + [vmem] * (2 + NY + 1),
    )(index, mine, other, *all_attn, terms)
    ring = Ring(terms)
    for _ in range(4):
        ring.step()
    grad_attn, grad_ssm = call(
        total_kernel, (shape((160, 256), F32), shape((160, 512), F32)), cost(0, 2**20)
    )(ring.right, ring.left, terms[0])
    return mixed, grad_attn, grad_ssm


def solution(mesh):
    fine = Mesh(mesh.devices.reshape(NY, NZ, NX, NC), ("y", "z", "x", "c"))
    tp = ("x", "c")
    both = P(YZ, tp)
    placed = (P(),) + (both,) * 8 + (P(tp), P(tp), P(tp, None), P(tp, None), both)
    return jax.shard_map(
        body, mesh=fine, in_specs=placed, out_specs=(both, both, both), check_vma=False
    )
```
